32 devices in a mesh: rep: 8 (over z, x), fsdp: 4 (over y, core).
Axes of the slice: x: 2, y: 2, z: 4, core: 2. Of those that a mesh axis runs over, the one named last changes fastest.
Arguments:
- partial_grads: bfloat16 [32, 512, 8192], P(('rep', 'fsdp')), may hold values from -6 to 6
- momentum: float32 [4096, 8192], P('rep', 'fsdp'), may hold values from -6 to 6
- freq_index: int32 [8, 8, 128, 32], P('rep', None, 'fsdp'), may hold values from 0 to 4095, all different within a row
Outputs:
- new_momentum: float32 [4096, 8192], P('rep', 'fsdp')
- update: float32 [512, 8192], P(None, 'fsdp')
The draws below stay inside these ranges and needn't reach their ends.
Inputs may be any that keep to these rules, and one draw needn't show every extreme that they name: `freq_index`: the 32 frequencies of one block of one replica are distinct.
All inputs are finite; a program needn't handle non-finite values.
Results may differ from the reference program's by a relative error of at most 0.0003.
Values may be sent and summed in bfloat16 or wider, within the bound.
A program may use at most 128 MiB of HBM per device.

```python
import jax
import jax.numpy as jnp
from jax import lax

D = 8192
ROWS = 512
GROUP = 64
K = 32
N_REP = 8
N_FSDP = 4


def with_spikes(entries, rng, source, target, shards_of, factor):
    owner, partner = [(jnp.arange(entries.shape[dim]) // (entries.shape[dim] // shards_of)).reshape([-1 if axis == dim else 1 for axis in range(entries.ndim)]) for dim in (source, target)]
    chosen = jax.random.permutation(rng, shards_of)[partner]
    strong = (owner == chosen) | (owner == (partner + shards_of // 2) % shards_of)
    return jnp.where(strong, factor * entries, entries)


def block_scale(own_key, shape, split, least, high):
    def one(dim, shards_of):
        heights = jax.random.uniform(jax.random.fold_in(jax.random.fold_in(own_key, 6), dim), (shards_of,), jnp.float32, least / len(split), high / len(split))
        return jnp.repeat(jnp.exp(heights), shape[dim] // shards_of).reshape((-1,) + (1,) * (len(shape) - dim - 1))

    gain = one(*split[0])
    for cut in split[1:]:
        gain = gain * one(*cut)
    return gain


def choose_distinct(rng, rows, number_of, top, lift):
    order = jax.random.permutation(jax.random.fold_in(rng, 1), number_of)
    boost = order
    for power in range(3):
        boost = boost * boost // number_of
    boost = boost * lift // number_of
    tickets = jax.random.randint(jax.random.fold_in(rng, 2), (rows, number_of), 0, 4096) + boost
    holders = jax.random.permutation(jax.random.fold_in(rng, 3), rows)[jnp.arange(number_of) % rows]
    tickets = jnp.where(jnp.arange(rows)[:, None] == holders[None, :], 1 << 14, tickets)
    priority = tickets * number_of + jnp.arange(number_of)
    return lax.top_k(priority.astype(jnp.int32), top)[1].astype(jnp.int32)


def normal_values(rng, dims, scale, bound, shards=(), held_as=jnp.bfloat16):
    entries = scale * jax.random.normal(rng, dims, jnp.float32)
    if shards:
        entries = entries * block_scale(rng, dims, shards, -0.22, 0.18)
    return jnp.clip(entries, -bound, bound).astype(held_as)


def noise_with(stream_key, shape, width, bound, shards, heavy, kind=jnp.bfloat16):
    result = width * jax.random.normal(stream_key, shape, jnp.float32)
    if shards:
        result = result * block_scale(stream_key, shape, shards, -0.22, 0.18)
    return jnp.clip(with_spikes(result, jax.random.fold_in(stream_key, 3), *heavy), -bound, bound).astype(kind)


def setup_inputs(seed: int = 0) -> dict:
    streams_of = jax.random.split(jax.random.key(seed), 4)
    return {
        "partial_grads": noise_with(streams_of[0], (N_REP * N_FSDP, ROWS, D), 0.5, 6.0, ((0, 32),), (0, 2, 32, 2.75)),
        "momentum": normal_values(streams_of[1], (N_REP * ROWS, D), 1.0, 6.0, ((0, 8), (1, 4)), jnp.float32),
        "freq_index": choose_distinct(streams_of[2], N_REP * (ROWS // GROUP) * (D // GROUP), GROUP * GROUP, K, 0).reshape((N_REP, ROWS // GROUP, D // GROUP, K)),
    }


momentum_decay = 0.9

def dct_basis(order):
    freq = jnp.arange(order, dtype=jnp.int32)[:, None]
    place = jnp.arange(order, dtype=jnp.int32)[None, :]
    phase = (2 * place + 1) * freq % (4 * order)
    scaling = jnp.where(freq == 0, jnp.sqrt(jnp.float32(1.0) / order), jnp.sqrt(jnp.float32(2.0) / order))
    return scaling * jnp.cos(jnp.pi * phase.astype(jnp.float32) / (2.0 * order))

def forward_blocks(field, basis, order):
    row_blocks = field.shape[0] // order
    col_blocks = field.shape[1] // order
    blocks = field.reshape(row_blocks, order, col_blocks, order)
    coef = jnp.einsum('kn,anbm,lm->abkl', basis, blocks, basis, precision=lax.Precision.HIGHEST)
    return coef.reshape(row_blocks, col_blocks, order * order)

def inverse_blocks(coef, basis, order):
    row_blocks, col_blocks = (coef.shape[0], coef.shape[1])
    square = coef.reshape(row_blocks, col_blocks, order, order)
    field = jnp.einsum('kn,abkl,lm->anbm', basis, square, basis, precision=lax.Precision.HIGHEST)
    return field.reshape(row_blocks * order, col_blocks * order)

def place_dense(values, positions, freqs):
    row_blocks, col_blocks = (values.shape[0], values.shape[1])
    row_ids = jnp.arange(row_blocks, dtype=jnp.int32)[:, None, None]
    col_ids = jnp.arange(col_blocks, dtype=jnp.int32)[None, :, None]
    empty = jnp.zeros((row_blocks, col_blocks, freqs), values.dtype)
    return empty.at[row_ids, col_ids, positions.astype(jnp.int32)].add(values)

def reference(partial_grads, momentum, freq_index):
    basis = dct_basis(GROUP)
    grads = partial_grads.astype(jnp.float32).reshape(N_REP, N_FSDP, ROWS, D).sum(axis=1)
    moment = momentum_decay * momentum.reshape(N_REP, ROWS, D) + grads

    def per_replica(pair):
        field, positions = pair
        coef = forward_blocks(field, basis, GROUP)
        kept = jnp.take_along_axis(coef, positions.astype(jnp.int32), axis=2)
        dense = place_dense(kept, positions, GROUP * GROUP)
        return (field - inverse_blocks(dense, basis, GROUP), dense)
    fresh, dense = lax.map(per_replica, (moment, freq_index))
    update = inverse_blocks(dense.sum(axis=0), basis, GROUP)
    return (fresh.reshape(N_REP * ROWS, D), update)
```

```python
import functools

import jax
import jax.numpy as jnp
import ml_dtypes
import numpy as np
from jax import lax
from jax.experimental import pallas as pl
from jax.experimental.pallas import tpu as pltpu
from jax.sharding import PartitionSpec as P

ORDER = 64
PACK = 4
WIDE = PACK * ORDER
MOMENTUM_DECAY = 0.9
MESH = pl.DeviceIdType.MESH
F32 = jnp.float32
BF16 = jnp.bfloat16
LEVELS = 32767.0


def constants():
    k = np.arange(ORDER)[:, None]
    n = np.arange(ORDER)[None, :]
    scale = np.where(k == 0, np.sqrt(1.0 / ORDER), np.sqrt(2.0 / ORDER))
    basis = (scale * np.cos(np.pi * ((2 * n + 1) * k % (4 * ORDER)) / (2.0 * ORDER))).astype(np.float32)

    def halves(matrix):
        high = matrix.astype(ml_dtypes.bfloat16)
        low = (matrix - high.astype(np.float32)).astype(ml_dtypes.bfloat16)
        return high, low

    def left(matrix):
        high, low = halves(matrix)
        return np.concatenate([high, low, high, np.zeros_like(high)], axis=1)

    eye = np.eye(PACK, dtype=np.float32)
    stack = [*halves(np.kron(eye, basis.T)), *halves(np.kron(eye, basis)), left(basis), left(basis.T)]
    return np.concatenate([m.astype(np.float32) for m in stack], axis=0)


def halves(x):
    high = x.astype(BF16)
    low = (x - high.astype(F32)).astype(BF16)
    return high, low


def mm(a, b):
    return lax.dot_general(a, b, (((1,), (0,)), ((), ())), preferred_element_type=F32)


def mm_nt(a, b):
    return lax.dot_general(a, b, (((1,), (1,)), ((), ())), preferred_element_type=F32)


def right_times(x, w_high, w_low):
    high, low = halves(x)
    both = mm(jnp.concatenate([high, low], axis=0), w_high)
    return both[:ORDER] + both[ORDER:] + mm(high, w_low)


def left_times(w, x):
    high, low = halves(x)
    return mm(w, jnp.concatenate([high, high, low], axis=0))


def hot_columns(pos, keep):
    lanes = pos.shape[1]
    lane = lax.broadcasted_iota(jnp.int32, (1, lanes), 1)
    block = lax.rem(lane, keep * PACK) // keep
    spot = block * ORDER + jnp.bitwise_and(pos, ORDER - 1)
    rows = lax.broadcasted_iota(jnp.int32, (WIDE, lanes), 0)
    return jnp.where(rows == spot, 1.0, 0.0).astype(BF16)


def hot_rows(pos):
    rows = lax.broadcasted_iota(jnp.int32, (ORDER, pos.shape[1]), 0)
    return rows == jnp.right_shift(pos, 6)


def kernel(
    nr, nq, na, ng, width, keep,
    pg, mom, idx, table, nm_out, up_out,
    wide_table, rf_high, rf_low, ri_high, ri_low, left_fwd, left_inv, table_sem,
    gbuf, pbuf, sbuf, rbuf, sscale, rscale, mbuf, ubuf, gidx, gval,
    own_sem, mom_sem, nm_sem, up_sem, pair_send, pair_recv,
    y_send, y_recv, ys_send, ys_recv, idx_send, idx_recv, val_send, val_recv,
):
    rep = lax.axis_index("rep")
    me = lax.axis_index("fsdp")
    chip = me // 2
    core = lax.rem(me, 2)
    partner = 2 * chip + 1 - core

    def rep_at(d):
        return lax.rem(rep + d, nr)

    def chip_at(d):
        return lax.rem(chip + d, nq)

    def rows(a):
        return pl.ds(pl.multiple_of(a * ORDER, ORDER), ORDER)

    def part(d, a, c):
        col = pl.multiple_of((2 * chip_at(d) + c) * width, width)
        return pg.at[0, rows(a), pl.ds(col, width)]

    def own_copy(d, a):
        return pltpu.make_async_copy(part(d, a, core), gbuf.at[d, a], own_sem.at[d, a])

    def mom_copy(a):
        return pltpu.make_async_copy(mom.at[rows(a), :], mbuf.at[a], mom_sem.at[a])

    def nm_copy(a):
        return pltpu.make_async_copy(mbuf.at[a], nm_out.at[rows(a), :], nm_sem.at[a])

    def up_copy(a):
        return pltpu.make_async_copy(ubuf.at[a], up_out.at[rows(a), :], up_sem.at[a])

    def pair_copy(d, a):
        return pltpu.make_async_remote_copy(
            part(d, a, 1 - core), pbuf.at[d, a], pair_send.at[d, a], pair_recv.at[d, a],
            device_id=(rep, partner), device_id_type=MESH)

    def y_copy(d, a):
        return pltpu.make_async_remote_copy(
            sbuf.at[d - 1, a], rbuf.at[d - 1, a], y_send.at[d - 1, a], y_recv.at[d - 1, a],
            device_id=(rep, 2 * chip_at(d) + core), device_id_type=MESH)

    def ys_copy(d, a):
        return pltpu.make_async_remote_copy(
            sscale.at[d - 1, a], rscale.at[d - 1, a], ys_send.at[d - 1, a], ys_recv.at[d - 1, a],
            device_id=(rep, 2 * chip_at(d) + core), device_id_type=MESH)

    def idx_copy(d):
        return pltpu.make_async_remote_copy(
            idx, gidx.at[d], idx_send.at[d], idx_recv.at[d],
            device_id=(rep_at(d), me), device_id_type=MESH)

    def val_copy(d, a):
        return pltpu.make_async_remote_copy(
            gval.at[0, a], gval.at[d, a], val_send.at[d, a], val_recv.at[d, a],
            device_id=(rep_at(d), me), device_id_type=MESH)

    def each(count, body):
        def step(i, carry):
            body(i)
            return carry
        lax.fori_loop(0, count, step, 0)

    table_copy = pltpu.make_async_copy(table, wide_table, table_sem)
    table_copy.start()

    def start_local(a):
        for d in range(1, nq):
            own_copy(d, a).start()
    each(na, start_local)

    barrier = pltpu.get_barrier_semaphore()
    pl.semaphore_signal(barrier, inc=1, device_id=(rep, partner), device_id_type=MESH)
    for d in range(1, nq):
        pl.semaphore_signal(barrier, inc=1, device_id=(rep, 2 * chip_at(d) + core), device_id_type=MESH)
    for d in range(1, nr):
        pl.semaphore_signal(barrier, inc=1, device_id=(rep_at(d), me), device_id_type=MESH)
    pl.semaphore_wait(barrier, nq + nr - 1)

    def start_pairs(a):
        for d in range(1, nq):
            pair_copy(d, a).start()
    each(na, start_pairs)

    def start_rest(a):
        pair_copy(0, a).start()
        own_copy(0, a).start()
        mom_copy(a).start()
    each(na, start_rest)

    def send_sums(a):
        for d in range(1, nq):
            own_copy(d, a).wait()
            pair_copy(d, a).wait_recv()

            def encode(g):
                cols = pl.ds(pl.multiple_of(g * WIDE, WIDE), WIDE)
                total = gbuf[d, a, :, cols].astype(F32) + pbuf[d, a, :, cols].astype(F32)
                top = jnp.maximum(jnp.max(jnp.abs(total), axis=0, keepdims=True), 1e-30)
                sscale[d - 1, a, :, cols] = top * (1.0 / LEVELS)
                sbuf[d - 1, a, :, cols] = jnp.round(total * (LEVELS / top)).astype(jnp.int32).astype(jnp.int16)
            each(ng, encode)
            y_copy(d, a).start()
            ys_copy(d, a).start()
    each(na, send_sums)

    for d in range(1, nr):
        idx_copy(d).start()
    gidx[0] = idx[...]

    table_copy.wait()
    for i, target in enumerate((rf_high, rf_low, ri_high, ri_low)):
        target[...] = wide_table[i * WIDE:(i + 1) * WIDE, :].astype(BF16)
    for i, target in enumerate((left_fwd, left_inv)):
        start = 4 * WIDE + i * ORDER
        target[...] = wide_table[start:start + ORDER, 0:3 * ORDER].astype(BF16)

    def find_kept(a):
        own_copy(0, a).wait()
        pair_copy(0, a).wait_recv()
        mom_copy(a).wait()
        for d in range(1, nq):
            y_copy(d, a).wait_recv()
            ys_copy(d, a).wait_recv()

        def one(g):
            cols = pl.ds(pl.multiple_of(g * WIDE, WIDE), WIDE)
            field = gbuf[0, a, :, cols].astype(F32) + pbuf[0, a, :, cols].astype(F32)
            for d in range(1, nq):
                field += rbuf[d - 1, a, :, cols].astype(jnp.int32).astype(F32) * rscale[d - 1, a, :, cols]
            field += MOMENTUM_DECAY * mbuf[a, :, cols]
            mbuf[a, :, cols] = field
            coef = left_times(left_fwd[...], right_times(field, rf_high[...], rf_low[...]))
            pos = gidx[0, a, pl.ds(g, 1), :]
            high, low = halves(coef)
            picked = mm(jnp.concatenate([high, low], axis=0), hot_columns(pos, keep))
            picked = picked[:ORDER] + picked[ORDER:]
            kept = jnp.sum(jnp.where(hot_rows(pos), picked, 0.0), axis=0, keepdims=True)
            gval[0, a, pl.ds(g, 1), :] = kept
        each(ng, one)
        for d in range(1, nr):
            val_copy(d, a).start()

    def decode(pos, val):
        high, low = halves(val)
        hot = hot_rows(pos)
        placed = jnp.concatenate(
            [jnp.where(hot, high.astype(F32), 0.0).astype(BF16), jnp.where(hot, low.astype(F32), 0.0).astype(BF16)], axis=0)
        dense = mm_nt(placed, hot_columns(pos, keep))
        dense = dense[:ORDER] + dense[ORDER:]
        return left_times(left_inv[...], right_times(dense, ri_high[...], ri_low[...]))

    def remove_kept(a):
        def one(g):
            cols = pl.ds(pl.multiple_of(g * WIDE, WIDE), WIDE)
            row = pl.ds(g, 1)
            mbuf[a, :, cols] = mbuf[a, :, cols] - decode(gidx[0, a, row, :], gval[0, a, row, :])
        each(ng, one)
        nm_copy(a).start()

    def add_up(a):
        for d in range(1, nr):
            val_copy(d, a).wait_recv()

        def one(g):
            cols = pl.ds(pl.multiple_of(g * WIDE, WIDE), WIDE)
            row = pl.ds(g, 1)
            pos = jnp.concatenate([gidx[d, a, row, :] for d in range(nr)], axis=1)
            val = jnp.concatenate([gval[d, a, row, :] for d in range(nr)], axis=1)
            ubuf[a, :, cols] = decode(pos, val)
        each(ng, one)
        up_copy(a).start()

    find_kept(0)
    remove_kept(0)
    for d in range(1, nr):
        idx_copy(d).wait_recv()

    def step(i):
        find_kept(i + 1)
        remove_kept(i + 1)
        add_up(i)
    each(na - 1, step)
    add_up(na - 1)

    def drain(a):
        for d in range(nq):
            pair_copy(d, a).wait_send()
        for d in range(1, nq):
            y_copy(d, a).wait_send()
            ys_copy(d, a).wait_send()
        for d in range(1, nr):
            val_copy(d, a).wait_send()
        nm_copy(a).wait()
        up_copy(a).wait()
    each(na, drain)
    for d in range(1, nr):
        idx_copy(d).wait_send()


def local(nr, nf, partial_grads, momentum, freq_index):
    total_rows, width = momentum.shape
    na = total_rows // ORDER
    ng = width // WIDE
    nq = nf // 2
    keep = freq_index.shape[3]
    lanes = PACK * keep
    idx = freq_index.reshape(na, ng, lanes)
    table = jnp.asarray(constants())
    dma = pltpu.SemaphoreType.DMA
    vmem = pl.BlockSpec(memory_space=pltpu.VMEM)
    hbm = pl.BlockSpec(memory_space=pl.ANY)
    return pl.pallas_call(
        functools.partial(kernel, nr, nq, na, ng, width, keep),
        out_shape=(
            jax.ShapeDtypeStruct((total_rows, width), F32),
            jax.ShapeDtypeStruct((total_rows, width), F32),
        ),
        in_specs=[hbm, hbm, vmem, hbm],
        out_specs=(hbm, hbm),
        scratch_shapes=[
            pltpu.VMEM(table.shape, F32),
            pltpu.VMEM((WIDE, WIDE), BF16), pltpu.VMEM((WIDE, WIDE), BF16),
            pltpu.VMEM((WIDE, WIDE), BF16), pltpu.VMEM((WIDE, WIDE), BF16),
            pltpu.VMEM((ORDER, 3 * ORDER), BF16), pltpu.VMEM((ORDER, 3 * ORDER), BF16),
            dma,
            pltpu.VMEM((nq, na, ORDER, width), BF16),
            pltpu.VMEM((nq, na, ORDER, width), BF16),
            pltpu.VMEM((nq - 1, na, ORDER, width), jnp.int16),
            pltpu.VMEM((nq - 1, na, ORDER, width), jnp.int16),
            pltpu.VMEM((nq - 1, na, 1, width), F32),
            pltpu.VMEM((nq - 1, na, 1, width), F32),
            pltpu.VMEM((na, ORDER, width), F32),
            pltpu.VMEM((na, ORDER, width), F32),
            pltpu.VMEM((nr, na, ng, lanes), jnp.int32),
            pltpu.VMEM((nr, na, ng, lanes), F32),
            dma((nq, na)), dma((na,)), dma((na,)), dma((na,)),
            dma((nq, na)), dma((nq, na)),
            dma((nq - 1, na)), dma((nq - 1, na)), dma((nq - 1, na)), dma((nq - 1, na)),
            dma((nr,)), dma((nr,)), dma((nr, na)), dma((nr, na)),
        ],
        compiler_params=pltpu.CompilerParams(
            collective_id=0, has_side_effects=True, vmem_limit_bytes=50 * 1024 * 1024),
        cost_estimate=pl.CostEstimate(
            flops=20 * 10**9, bytes_accessed=28 * 2**20, transcendentals=0),
    )(partial_grads, momentum, idx, table)


def solution(mesh):
    return jax.shard_map(
        functools.partial(local, mesh.shape["rep"], mesh.shape["fsdp"]),
        mesh=mesh,
        in_specs=(P(("rep", "fsdp"), None, None), P("rep", "fsdp"), P("rep", None, "fsdp", None)),
        out_specs=(P("rep", "fsdp"), P(None, "fsdp")),
        check_vma=False,
    )
```

```python
import functools

import jax
import jax.numpy as jnp
import numpy as np
from jax import lax
from jax.experimental import pallas as pl
from jax.experimental.pallas import tpu as pltpu
from jax.sharding import PartitionSpec as P

ORDER = 64
PACK = 4
WIDE = PACK * ORDER
MOMENTUM_DECAY = 0.9
MESH = pl.DeviceIdType.MESH
F32 = jnp.float32
BF16 = jnp.bfloat16
LEVELS = 32767.0


def constants():
    k = np.arange(ORDER)[:, None]
    n = np.arange(ORDER)[None, :]
    scale = np.where(k == 0, np.sqrt(1.0 / ORDER), np.sqrt(2.0 / ORDER))
    basis = (scale * np.cos(np.pi * ((2 * n + 1) * k % (4 * ORDER)) / (2.0 * ORDER))).astype(np.float32)

    return np.tile(np.concatenate([basis.T, basis], axis=0), (1, PACK))


def halves(x):
    high = x.astype(BF16)
    low = (x - high.astype(F32)).astype(BF16)
    return high, low


def mm(a, b):
    return lax.dot_general(a, b, (((1,), (0,)), ((), ())), preferred_element_type=F32)


def mm_nt(a, b):
    return lax.dot_general(a, b, (((1,), (1,)), ((), ())), preferred_element_type=F32)


def right_times(x, w_high, w_low):
    high, low = halves(x)
    both = mm(jnp.concatenate([high, low], axis=0), w_high)
    return both[:ORDER] + both[ORDER:] + mm(high, w_low)


def left_times(w, x):
    high, low = halves(x)
    return mm(w, jnp.concatenate([high, high, low], axis=0))


def hot_columns(pos, keep):
    lanes = pos.shape[1]
    lane = lax.broadcasted_iota(jnp.int32, (1, lanes), 1)
    block = lax.rem(lane, keep * PACK) // keep
    spot = block * ORDER + jnp.bitwise_and(pos, ORDER - 1)
    rows = lax.broadcasted_iota(jnp.int32, (WIDE, lanes), 0)
    return jnp.where(rows == spot, 1.0, 0.0).astype(BF16)


def hot_rows(pos):
    rows = lax.broadcasted_iota(jnp.int32, (ORDER, pos.shape[1]), 0)
    return rows == jnp.right_shift(pos, 6)


def kernel(
    nr, nq, na, ng, width, keep,
    pg, mom, idx, table, mbuf, ubuf,
    rf_high, rf_low, ri_high, ri_low, left_fwd, left_inv,
    gbuf, pbuf, sbuf, rbuf, sscale, rscale, gidx, gval,
    own_sem, mom_sem, pair_send, pair_recv,
    y_send, y_recv, ys_send, ys_recv, idx_send, idx_recv, val_send, val_recv,
):
    rep = lax.axis_index("rep")
    me = lax.axis_index("fsdp")
    chip = me // 2
    core = lax.rem(me, 2)
    partner = 2 * chip + 1 - core

    def rep_at(d):
        return lax.rem(rep + d, nr)

    def chip_at(d):
        return lax.rem(chip + d, nq)

    def rows(a):
        return pl.ds(pl.multiple_of(a * ORDER, ORDER), ORDER)

    def part(d, a, c):
        col = pl.multiple_of((2 * chip_at(d) + c) * width, width)
        return pg.at[0, rows(a), pl.ds(col, width)]

    def own_copy(d, a):
        return pltpu.make_async_copy(part(d, a, core), gbuf.at[d, a], own_sem.at[d, a])

    def mom_copy(a):
        return pltpu.make_async_copy(mom.at[rows(a), :], mbuf.at[rows(a), :], mom_sem.at[a])

    def pair_copy(d, a):
        return pltpu.make_async_remote_copy(
            part(d, a, 1 - core), pbuf.at[d, a], pair_send.at[d, a], pair_recv.at[d, a],
            device_id=(rep, partner), device_id_type=MESH)

    def y_copy(d, a):
        return pltpu.make_async_remote_copy(
            sbuf.at[d - 1, a], rbuf.at[d - 1, a], y_send.at[d - 1, a], y_recv.at[d - 1, a],
            device_id=(rep, 2 * chip_at(d) + core), device_id_type=MESH)

    def ys_copy(d, a):
        return pltpu.make_async_remote_copy(
            sscale.at[d - 1, a], rscale.at[d - 1, a], ys_send.at[d - 1, a], ys_recv.at[d - 1, a],
            device_id=(rep, 2 * chip_at(d) + core), device_id_type=MESH)

    def idx_copy(d):
        return pltpu.make_async_remote_copy(
            idx, gidx.at[d], idx_send.at[d], idx_recv.at[d],
            device_id=(rep_at(d), me), device_id_type=MESH)

    def val_copy(d, a):
        return pltpu.make_async_remote_copy(
            gval.at[0, a], gval.at[d, a], val_send.at[d, a], val_recv.at[d, a],
            device_id=(rep_at(d), me), device_id_type=MESH)

    def each(count, body):
        def step(i, carry):
            body(i)
            return carry
        lax.fori_loop(0, count, step, 0)

    def start_local(a):
        for d in range(1, nq):
            own_copy(d, a).start()
    each(na, start_local)

    barrier = pltpu.get_barrier_semaphore()
    pl.semaphore_signal(barrier, inc=1, device_id=(rep, partner), device_id_type=MESH)
    for d in range(1, nq):
        pl.semaphore_signal(barrier, inc=1, device_id=(rep, 2 * chip_at(d) + core), device_id_type=MESH)
    for d in range(1, nr):
        pl.semaphore_signal(barrier, inc=1, device_id=(rep_at(d), me), device_id_type=MESH)
    pl.semaphore_wait(barrier, nq + nr - 1)

    def start_pairs(a):
        for d in range(1, nq):
            pair_copy(d, a).start()
    each(na, start_pairs)

    def start_rest(a):
        pair_copy(0, a).start()
        own_copy(0, a).start()
        mom_copy(a).start()
    each(na, start_rest)

    span = (2 if ng % 2 == 0 else 1) * WIDE

    def send_sums(a):
        for d in range(1, nq):
            own_copy(d, a).wait()
            pair_copy(d, a).wait_recv()

            def encode(g):
                cols = pl.ds(pl.multiple_of(g * span, span), span)
                total = gbuf[d, a, :, cols].astype(F32) + pbuf[d, a, :, cols].astype(F32)
                top = jnp.maximum(jnp.max(jnp.abs(total), axis=0, keepdims=True), 1e-30)
                sscale[d - 1, a, :, cols] = top * (1.0 / LEVELS)
                sbuf[d - 1, a, :, cols] = jnp.round(total * (LEVELS / top)).astype(jnp.int32).astype(jnp.int16)
            each(width // span, encode)
            y_copy(d, a).start()
            ys_copy(d, a).start()
    each(na, send_sums)

    for d in range(1, nr):
        idx_copy(d).start()
    gidx[0] = idx[...]

    def blocks_of(shape):
        row = lax.broadcasted_iota(jnp.int32, shape, 0) // ORDER
        return row, lax.broadcasted_iota(jnp.int32, shape, 1) // ORDER

    row_block, col_block = blocks_of((WIDE, WIDE))
    for i, (high, low) in enumerate(((rf_high, rf_low), (ri_high, ri_low))):
        tiled = table[i * ORDER:(i + 1) * ORDER, :]
        wide = jnp.where(row_block == col_block, jnp.concatenate([tiled] * PACK, axis=0), 0.0)
        high[...], low[...] = halves(wide)
    _, col_block = blocks_of((ORDER, WIDE))
    for i, target in enumerate((left_inv, left_fwd)):
        tiled = table[i * ORDER:(i + 1) * ORDER, :]
        high = tiled.astype(BF16).astype(F32)
        target[...] = jnp.where(col_block == 1, tiled - high, high).astype(BF16)[:, :3 * ORDER]

    for d in range(1, nr):
        idx_copy(d).wait_recv()

    ways = 4 if ng % 4 == 0 else (2 if ng % 2 == 0 else 1)

    def groups(body):
        def some(i):
            gs = [i * ways + w for w in range(ways)]
            body(gs, [pl.ds(pl.multiple_of(g * WIDE, WIDE), WIDE) for g in gs], [pl.ds(g, 1) for g in gs])
        each(ng // ways, some)

    def right_all(xs, w_high, w_low):
        split = [halves(x) for x in xs]
        high = jnp.concatenate([h for h, _ in split], axis=0)
        low = jnp.concatenate([l for _, l in split], axis=0)
        out = mm(high, w_high) + (mm(low, w_high) + mm(high, w_low))
        return [out[w * ORDER:(w + 1) * ORDER] for w in range(len(xs))]

    def find_kept(a):
        own_copy(0, a).wait()
        pair_copy(0, a).wait_recv()
        mom_copy(a).wait()
        for d in range(1, nq):
            y_copy(d, a).wait_recv()
            ys_copy(d, a).wait_recv()

        def some(gs, cols, row):
            field = [gbuf[0, a, :, c].astype(F32) + pbuf[0, a, :, c].astype(F32) for c in cols]
            for d in range(1, nq):
                field = [f + rbuf[d - 1, a, :, c].astype(jnp.int32).astype(F32) * rscale[d - 1, a, :, c]
                         for f, c in zip(field, cols)]
            field = [f + MOMENTUM_DECAY * mbuf[rows(a), c] for f, c in zip(field, cols)]
            pos = [gidx[0, a, r, :] for r in row]
            for f, c in zip(field, cols):
                mbuf[rows(a), c] = f
            half = right_all(field, rf_high[...], rf_low[...])
            coef = [halves(left_times(left_fwd[...], h)) for h in half]
            picked = [mm(jnp.concatenate(c, axis=0), hot_columns(p, keep)) for c, p in zip(coef, pos)]
            kept = [jnp.sum(jnp.where(hot_rows(p), x[:ORDER] + x[ORDER:], 0.0), axis=0, keepdims=True)
                    for x, p in zip(picked, pos)]
            for r, k in zip(row, kept):
                gval[0, a, r, :] = k
        groups(some)
        for d in range(1, nr):
            val_copy(d, a).start()

    def decode(pos, val):
        dense = []
        for p, v in zip(pos, val):
            high, low = halves(v)
            hot = hot_rows(p)
            placed = jnp.concatenate(
                [jnp.where(hot, x.astype(F32), 0.0).astype(BF16) for x in (high, low)], axis=0)
            both = mm_nt(placed, hot_columns(p, keep))
            dense.append(both[:ORDER] + both[ORDER:])
        half = right_all(dense, ri_high[...], ri_low[...])
        return [left_times(left_inv[...], h) for h in half]

    def remove_kept(a):
        def some(gs, cols, row):
            field = [mbuf[rows(a), c] for c in cols]
            part = decode([gidx[0, a, r, :] for r in row], [gval[0, a, r, :] for r in row])
            for f, x, c in zip(field, part, cols):
                mbuf[rows(a), c] = f - x
        groups(some)

    def add_up(a):
        for d in range(1, nr):
            val_copy(d, a).wait_recv()

        def some(gs, cols, row):
            pos = [jnp.concatenate([gidx[d, a, r, :] for d in range(nr)], axis=1) for r in row]
            val = [jnp.concatenate([gval[d, a, r, :] for d in range(nr)], axis=1) for r in row]
            for x, c in zip(decode(pos, val), cols):
                ubuf[rows(a), c] = x
        groups(some)

    def step(i):
        @pl.when(i < na)
        def _():
            find_kept(i)
            remove_kept(i)

        @pl.when(i > 0)
        def _():
            add_up(i - 1)
    each(na + 1, step)

    def drain(a):
        for d in range(nq):
            pair_copy(d, a).wait_send()
        for d in range(1, nq):
            y_copy(d, a).wait_send()
            ys_copy(d, a).wait_send()
        for d in range(1, nr):
            val_copy(d, a).wait_send()
    each(na, drain)
    for d in range(1, nr):
        idx_copy(d).wait_send()


def local(nr, nf, partial_grads, momentum, freq_index):
    total_rows, width = momentum.shape
    na = total_rows // ORDER
    ng = width // WIDE
    nq = nf // 2
    keep = freq_index.shape[3]
    lanes = PACK * keep
    idx = freq_index.reshape(na, ng, lanes)
    table = jnp.asarray(constants())
    dma = pltpu.SemaphoreType.DMA
    vmem = pl.BlockSpec(memory_space=pltpu.VMEM)
    hbm = pl.BlockSpec(memory_space=pltpu.HBM)
    return pl.pallas_call(
        functools.partial(kernel, nr, nq, na, ng, width, keep),
        out_shape=(
            jax.ShapeDtypeStruct((total_rows, width), F32),
            jax.ShapeDtypeStruct((total_rows, width), F32),
        ),
        in_specs=[hbm, hbm, vmem, vmem],
        out_specs=(vmem, vmem),
        scratch_shapes=[
            pltpu.VMEM((WIDE, WIDE), BF16), pltpu.VMEM((WIDE, WIDE), BF16),
            pltpu.VMEM((WIDE, WIDE), BF16), pltpu.VMEM((WIDE, WIDE), BF16),
            pltpu.VMEM((ORDER, 3 * ORDER), BF16), pltpu.VMEM((ORDER, 3 * ORDER), BF16),
            pltpu.VMEM((nq, na, ORDER, width), BF16),
            pltpu.VMEM((nq, na, ORDER, width), BF16),
            pltpu.VMEM((nq - 1, na, ORDER, width), jnp.int16),
            pltpu.VMEM((nq - 1, na, ORDER, width), jnp.int16),
            pltpu.VMEM((nq - 1, na, 1, width), F32),
            pltpu.VMEM((nq - 1, na, 1, width), F32),
            pltpu.VMEM((nr, na, ng, lanes), jnp.int32),
            pltpu.VMEM((nr, na, ng, lanes), F32),
            dma((nq, na)), dma((na,)),
            dma((nq, na)), dma((nq, na)),
            dma((nq - 1, na)), dma((nq - 1, na)), dma((nq - 1, na)), dma((nq - 1, na)),
            dma((nr,)), dma((nr,)), dma((nr, na)), dma((nr, na)),
        ],
        compiler_params=pltpu.CompilerParams(
            collective_id=0, has_side_effects=True, vmem_limit_bytes=43 * 1024 * 1024),
        cost_estimate=pl.CostEstimate(
            flops=20 * 10**9, bytes_accessed=28 * 2**20, transcendentals=0),
    )(partial_grads, momentum, idx, table)


def solution(mesh):
    return jax.shard_map(
        functools.partial(local, mesh.shape["rep"], mesh.shape["fsdp"]),
        mesh=mesh,
        in_specs=(P(("rep", "fsdp"), None, None), P("rep", "fsdp"), P("rep", None, "fsdp", None)),
        out_specs=(P("rep", "fsdp"), P(None, "fsdp")),
        check_vma=False,
    )
```

```python
import functools
import math

import jax
import jax.numpy as jnp
from jax import lax
from jax.experimental import pallas as pl
from jax.experimental.pallas import tpu as pltpu
from jax.sharding import PartitionSpec as P

ORDER = 64
PACK = 4
WIDE = PACK * ORDER
MOMENTUM_DECAY = 0.9
MESH = pl.DeviceIdType.MESH
F32 = jnp.float32
BF16 = jnp.bfloat16
LEVELS = 32767.0


def tiled_basis(transposed):
    row = lax.broadcasted_iota(jnp.int32, (ORDER, WIDE), 0)
    lane = jnp.bitwise_and(lax.broadcasted_iota(jnp.int32, (ORDER, WIDE), 1), ORDER - 1)
    freq, place = (lane, row) if transposed else (row, lane)
    turn = jnp.bitwise_and((2 * place + 1) * freq, 4 * ORDER - 1)
    x = (jnp.abs(turn - 2 * ORDER) - ORDER).astype(F32) * (math.pi / (2 * ORDER))
    square = x * x
    series = jnp.ones_like(x)
    for power in (14, 12, 10, 8, 6, 4, 2):
        series = 1.0 - square * series * (1.0 / (power * (power + 1)))
    return jnp.where(freq == 0, math.sqrt(1.0 / ORDER), math.sqrt(2.0 / ORDER)) * (x * series)


def halves(x):
    high = x.astype(BF16)
    low = (x - high.astype(F32)).astype(BF16)
    return high, low


def mm(a, b):
    return lax.dot_general(a, b, (((1,), (0,)), ((), ())), preferred_element_type=F32)


def mm_nt(a, b):
    return lax.dot_general(a, b, (((1,), (1,)), ((), ())), preferred_element_type=F32)


def right_times(x, w_high, w_low):
    high, low = halves(x)
    both = mm(jnp.concatenate([high, low], axis=0), w_high)
    return both[:ORDER] + both[ORDER:] + mm(high, w_low)


def left_times(w, x):
    high, low = halves(x)
    return mm(w, jnp.concatenate([high, high, low], axis=0))


def hot_columns(pos, keep):
    lanes = pos.shape[1]
    lane = lax.broadcasted_iota(jnp.int32, (1, lanes), 1)
    block = lax.rem(lane, keep * PACK) // keep
    spot = block * ORDER + jnp.bitwise_and(pos, ORDER - 1)
    rows = lax.broadcasted_iota(jnp.int32, (WIDE, lanes), 0)
    return jnp.where(rows == spot, 1.0, 0.0).astype(BF16)


def hot_rows(pos):
    rows = lax.broadcasted_iota(jnp.int32, (ORDER, pos.shape[1]), 0)
    return rows == jnp.right_shift(pos, 6)


def kernel(
    nr, nq, na, ng, width, keep,
    pg, mom, idx, mbuf, ubuf,
    rf_high, rf_low, ri_high, ri_low, left_fwd, left_inv,
    gbuf, pbuf, sbuf, rbuf, sscale, rscale, gidx, gval,
    own_sem, mom_sem, pair_send, pair_recv,
    y_send, y_recv, ys_send, ys_recv, idx_send, idx_recv, val_send, val_recv,
):
    rep = lax.axis_index("rep")
    me = lax.axis_index("fsdp")
    chip = me // 2
    core = lax.rem(me, 2)
    partner = 2 * chip + 1 - core

    def rep_at(d):
        return lax.rem(rep + d, nr)

    def chip_at(d):
        return lax.rem(chip + d, nq)

    def rows(a):
        return pl.ds(pl.multiple_of(a * ORDER, ORDER), ORDER)

    def part(d, a, c):
        col = pl.multiple_of((2 * chip_at(d) + c) * width, width)
        return pg.at[0, rows(a), pl.ds(col, width)]

    def own_copy(d, a):
        return pltpu.make_async_copy(part(d, a, core), gbuf.at[d, a], own_sem.at[d, a])

    def mom_copy(a):
        return pltpu.make_async_copy(mom.at[rows(a), :], mbuf.at[rows(a), :], mom_sem.at[a])

    def pair_copy(d, a):
        return pltpu.make_async_remote_copy(
            part(d, a, 1 - core), pbuf.at[d, a], pair_send.at[d, a], pair_recv.at[d, a],
            device_id=(rep, partner), device_id_type=MESH)

    def y_copy(d, a):
        return pltpu.make_async_remote_copy(
            sbuf.at[d - 1, a], rbuf.at[d - 1, a], y_send.at[d - 1, a], y_recv.at[d - 1, a],
            device_id=(rep, 2 * chip_at(d) + core), device_id_type=MESH)

    def ys_copy(d, a):
        return pltpu.make_async_remote_copy(
            sscale.at[d - 1, a], rscale.at[d - 1, a], ys_send.at[d - 1, a], ys_recv.at[d - 1, a],
            device_id=(rep, 2 * chip_at(d) + core), device_id_type=MESH)

    def idx_copy(d):
        return pltpu.make_async_remote_copy(
            idx, gidx.at[d], idx_send.at[d], idx_recv.at[d],
            device_id=(rep_at(d), me), device_id_type=MESH)

    def val_copy(d, a):
        return pltpu.make_async_remote_copy(
            gval.at[0, a], gval.at[d, a], val_send.at[d, a], val_recv.at[d, a],
            device_id=(rep_at(d), me), device_id_type=MESH)

    def each(count, body):
        def step(i, carry):
            body(i)
            return carry
        lax.fori_loop(0, count, step, 0)

    def start_local(a):
        for d in range(1, nq):
            own_copy(d, a).start()
    each(na, start_local)

    barrier = pltpu.get_barrier_semaphore()
    pl.semaphore_signal(barrier, inc=1, device_id=(rep, partner), device_id_type=MESH)
    for d in range(1, nq):
        pl.semaphore_signal(barrier, inc=1, device_id=(rep, 2 * chip_at(d) + core), device_id_type=MESH)
    for d in range(1, nr):
        pl.semaphore_signal(barrier, inc=1, device_id=(rep_at(d), me), device_id_type=MESH)
    pl.semaphore_wait(barrier, nq + nr - 1)

    def start_pairs(a):
        for d in range(1, nq):
            pair_copy(d, a).start()
    each(na, start_pairs)

    def start_rest(a):
        pair_copy(0, a).start()
        own_copy(0, a).start()
        mom_copy(a).start()
    each(na, start_rest)

    span = (2 if ng % 2 == 0 else 1) * WIDE

    def send_sums(a):
        for d in range(1, nq):
            own_copy(d, a).wait()
            pair_copy(d, a).wait_recv()

            def encode(g):
                cols = pl.ds(pl.multiple_of(g * span, span), span)
                total = gbuf[d, a, :, cols].astype(F32) + pbuf[d, a, :, cols].astype(F32)
                top = jnp.maximum(jnp.max(jnp.abs(total), axis=0, keepdims=True), 1e-30)
                sscale[d - 1, a, :, cols] = top * (1.0 / LEVELS)
                sbuf[d - 1, a, :, cols] = jnp.round(total * (LEVELS / top)).astype(jnp.int32).astype(jnp.int16)
            each(width // span, encode)
            y_copy(d, a).start()
            ys_copy(d, a).start()
    each(na, send_sums)

    for d in range(1, nr):
        idx_copy(d).start()
    gidx[0] = idx[...]

    def blocks_of(shape):
        row = lax.broadcasted_iota(jnp.int32, shape, 0) // ORDER
        return row, lax.broadcasted_iota(jnp.int32, shape, 1) // ORDER

    row_block, col_block = blocks_of((WIDE, WIDE))
    for i, (high, low) in enumerate(((rf_high, rf_low), (ri_high, ri_low))):
        tiled = tiled_basis(i == 0)
        wide = jnp.where(row_block == col_block, jnp.concatenate([tiled] * PACK, axis=0), 0.0)
        high[...], low[...] = halves(wide)
    _, col_block = blocks_of((ORDER, WIDE))
    for i, target in enumerate((left_inv, left_fwd)):
        tiled = tiled_basis(i == 0)
        high = tiled.astype(BF16).astype(F32)
        target[...] = jnp.where(col_block == 1, tiled - high, high).astype(BF16)[:, :3 * ORDER]

    for d in range(1, nr):
        idx_copy(d).wait_recv()

    ways = max(w for w in (1, 2, 4, 8) if ng % w == 0)

    def groups(body):
        def some(i):
            gs = [i * ways + w for w in range(ways)]
            body(gs, [pl.ds(pl.multiple_of(g * WIDE, WIDE), WIDE) for g in gs], [pl.ds(g, 1) for g in gs])
        each(ng // ways, some)

    def right_all(xs, w_high, w_low):
        split = [halves(x) for x in xs]
        high = jnp.concatenate([h for h, _ in split], axis=0)
        low = jnp.concatenate([l for _, l in split], axis=0)
        out = mm(high, w_high) + (mm(low, w_high) + mm(high, w_low))
        return [out[w * ORDER:(w + 1) * ORDER] for w in range(len(xs))]

    def find_kept(a):
        own_copy(0, a).wait()
        pair_copy(0, a).wait_recv()
        mom_copy(a).wait()
        for d in range(1, nq):
            y_copy(d, a).wait_recv()
            ys_copy(d, a).wait_recv()

        def some(gs, cols, row):
            field = [gbuf[0, a, :, c].astype(F32) + pbuf[0, a, :, c].astype(F32) for c in cols]
            for d in range(1, nq):
                field = [f + rbuf[d - 1, a, :, c].astype(jnp.int32).astype(F32) * rscale[d - 1, a, :, c]
                         for f, c in zip(field, cols)]
            field = [f + MOMENTUM_DECAY * mbuf[rows(a), c] for f, c in zip(field, cols)]
            pos = [gidx[0, a, r, :] for r in row]
            for f, c in zip(field, cols):
                mbuf[rows(a), c] = f
            half = right_all(field, rf_high[...], rf_low[...])
            coef = [halves(left_times(left_fwd[...], h)) for h in half]
            picked = [mm(jnp.concatenate(c, axis=0), hot_columns(p, keep)) for c, p in zip(coef, pos)]
            kept = [jnp.sum(jnp.where(hot_rows(p), x[:ORDER] + x[ORDER:], 0.0), axis=0, keepdims=True)
                    for x, p in zip(picked, pos)]
            for r, k in zip(row, kept):
                gval[0, a, r, :] = k
        groups(some)
        for d in range(1, nr):
            val_copy(d, a).start()

    def decode(pos, val):
        dense = []
        for p, v in zip(pos, val):
            high, low = halves(v)
            hot = hot_rows(p)
            placed = jnp.concatenate(
                [jnp.where(hot, x.astype(F32), 0.0).astype(BF16) for x in (high, low)], axis=0)
            both = mm_nt(placed, hot_columns(p, keep))
            dense.append(both[:ORDER] + both[ORDER:])
        half = right_all(dense, ri_high[...], ri_low[...])
        return [left_times(left_inv[...], h) for h in half]

    def remove_kept(a):
        def some(gs, cols, row):
            field = [mbuf[rows(a), c] for c in cols]
            part = decode([gidx[0, a, r, :] for r in row], [gval[0, a, r, :] for r in row])
            for f, x, c in zip(field, part, cols):
                mbuf[rows(a), c] = f - x
        groups(some)

    def add_up(a):
        for d in range(1, nr):
            val_copy(d, a).wait_recv()

        def some(gs, cols, row):
            pos = [jnp.concatenate([gidx[d, a, r, :] for d in range(nr)], axis=1) for r in row]
            val = [jnp.concatenate([gval[d, a, r, :] for d in range(nr)], axis=1) for r in row]
            for x, c in zip(decode(pos, val), cols):
                ubuf[rows(a), c] = x
        groups(some)

    def step(i):
        @pl.when(i > 0)
        def _():
            add_up(i - 1)

        @pl.when(i < na)
        def _():
            find_kept(i)
            remove_kept(i)
    each(na + 1, step)

    def drain(a):
        for d in range(nq):
            pair_copy(d, a).wait_send()
        for d in range(1, nq):
            y_copy(d, a).wait_send()
            ys_copy(d, a).wait_send()
        for d in range(1, nr):
            val_copy(d, a).wait_send()
    each(na, drain)
    for d in range(1, nr):
        idx_copy(d).wait_send()


def local(nr, nf, partial_grads, momentum, freq_index):
    total_rows, width = momentum.shape
    na = total_rows // ORDER
    ng = width // WIDE
    nq = nf // 2
    keep = freq_index.shape[3]
    lanes = PACK * keep
    idx = freq_index.reshape(na, ng, lanes)
    dma = pltpu.SemaphoreType.DMA
    vmem = pl.BlockSpec(memory_space=pltpu.VMEM)
    hbm = pl.BlockSpec(memory_space=pltpu.HBM)
    return pl.pallas_call(
        functools.partial(kernel, nr, nq, na, ng, width, keep),
        out_shape=(
            jax.ShapeDtypeStruct((total_rows, width), F32),
            jax.ShapeDtypeStruct((total_rows, width), F32),
        ),
        in_specs=[hbm, hbm, vmem],
        out_specs=(vmem, vmem),
        scratch_shapes=[
            pltpu.VMEM((WIDE, WIDE), BF16), pltpu.VMEM((WIDE, WIDE), BF16),
            pltpu.VMEM((WIDE, WIDE), BF16), pltpu.VMEM((WIDE, WIDE), BF16),
            pltpu.VMEM((ORDER, 3 * ORDER), BF16), pltpu.VMEM((ORDER, 3 * ORDER), BF16),
            pltpu.VMEM((nq, na, ORDER, width), BF16),
            pltpu.VMEM((nq, na, ORDER, width), BF16),
            pltpu.VMEM((nq - 1, na, ORDER, width), jnp.int16),
            pltpu.VMEM((nq - 1, na, ORDER, width), jnp.int16),
            pltpu.VMEM((nq - 1, na, 1, width), F32),
            pltpu.VMEM((nq - 1, na, 1, width), F32),
            pltpu.VMEM((nr, na, ng, lanes), jnp.int32),
            pltpu.VMEM((nr, na, ng, lanes), F32),
            dma((nq, na)), dma((na,)),
            dma((nq, na)), dma((nq, na)),
            dma((nq - 1, na)), dma((nq - 1, na)), dma((nq - 1, na)), dma((nq - 1, na)),
            dma((nr,)), dma((nr,)), dma((nr, na)), dma((nr, na)),
        ],
        compiler_params=pltpu.CompilerParams(
            collective_id=0, has_side_effects=True, vmem_limit_bytes=43 * 1024 * 1024),
        cost_estimate=pl.CostEstimate(
            flops=20 * 10**9, bytes_accessed=28 * 2**20, transcendentals=0),
    )(partial_grads, momentum, idx)


def solution(mesh):
    return jax.shard_map(
        functools.partial(local, mesh.shape["rep"], mesh.shape["fsdp"]),
        mesh=mesh,
        in_specs=(P(("rep", "fsdp"), None, None), P("rep", "fsdp"), P("rep", None, "fsdp", None)),
        out_specs=(P("rep", "fsdp"), P(None, "fsdp")),
        check_vma=False,
    )
```

```python
import functools
import math

import jax
import jax.numpy as jnp
from jax import lax
from jax.experimental import pallas as pl
from jax.experimental.pallas import tpu as pltpu
from jax.sharding import PartitionSpec as P

ORDER = 64
PACK = 4
WIDE = PACK * ORDER
MOMENTUM_DECAY = 0.9
MESH = pl.DeviceIdType.MESH
F32 = jnp.float32
BF16 = jnp.bfloat16
LEVELS = 32767.0


def tiled_basis(transposed):
    row = lax.broadcasted_iota(jnp.int32, (ORDER, WIDE), 0)
    lane = jnp.bitwise_and(lax.broadcasted_iota(jnp.int32, (ORDER, WIDE), 1), ORDER - 1)
    freq, place = (lane, row) if transposed else (row, lane)
    turn = jnp.bitwise_and((2 * place + 1) * freq, 4 * ORDER - 1)
    x = (jnp.abs(turn - 2 * ORDER) - ORDER).astype(F32) * (math.pi / (2 * ORDER))
    square = x * x
    series = jnp.ones_like(x)
    for power in (14, 12, 10, 8, 6, 4, 2):
        series = 1.0 - square * series * (1.0 / (power * (power + 1)))
    return jnp.where(freq == 0, math.sqrt(1.0 / ORDER), math.sqrt(2.0 / ORDER)) * (x * series)


def halves(x):
    high = x.astype(BF16)
    low = (x - high.astype(F32)).astype(BF16)
    return high, low


def mm(a, b):
    return lax.dot_general(a, b, (((1,), (0,)), ((), ())), preferred_element_type=F32)


def mm_nt(a, b):
    return lax.dot_general(a, b, (((1,), (1,)), ((), ())), preferred_element_type=F32)


def right_times(x, w_high, w_low):
    high, low = halves(x)
    both = mm(jnp.concatenate([high, low], axis=0), w_high)
    return both[:ORDER] + both[ORDER:] + mm(high, w_low)


def left_times(w, x):
    high, low = halves(x)
    return mm(w, jnp.concatenate([high, high, low], axis=0))


def hot_columns(pos, keep):
    lanes = pos.shape[1]
    lane = lax.broadcasted_iota(jnp.int32, (1, lanes), 1)
    block = lax.rem(lane, keep * PACK) // keep
    spot = block * ORDER + jnp.bitwise_and(pos, ORDER - 1)
    rows = lax.broadcasted_iota(jnp.int32, (WIDE, lanes), 0)
    return jnp.where(rows == spot, 1.0, 0.0).astype(BF16)


def hot_rows(pos):
    rows = lax.broadcasted_iota(jnp.int32, (ORDER, pos.shape[1]), 0)
    return rows == jnp.right_shift(pos, 6)


def kernel(
    nr, nq, na, ng, width, keep,
    pg, mom, idx, mbuf, ubuf,
    rf_high, rf_low, ri_high, ri_low, left_fwd, left_inv,
    gbuf, pbuf, sbuf, rbuf, sscale, rscale, gidx, gval,
    own_sem, mom_sem, pair_send, pair_recv,
    y_send, y_recv, ys_send, ys_recv, idx_send, idx_recv, val_send, val_recv,
):
    rep = lax.axis_index("rep")
    me = lax.axis_index("fsdp")
    chip = me // 2
    core = lax.rem(me, 2)
    partner = 2 * chip + 1 - core

    def rep_at(d):
        return lax.rem(rep + d, nr)

    def chip_at(d):
        return lax.rem(chip + d, nq)

    def rows(a):
        return pl.ds(pl.multiple_of(a * ORDER, ORDER), ORDER)

    def part(d, a, c):
        col = pl.multiple_of((2 * chip_at(d) + c) * width, width)
        return pg.at[0, rows(a), pl.ds(col, width)]

    def own_copy(d, a):
        return pltpu.make_async_copy(part(d, a, core), gbuf.at[d, a], own_sem.at[d, a])

    def mom_copy(a):
        return pltpu.make_async_copy(mom.at[rows(a), :], mbuf.at[rows(a), :], mom_sem.at[a])

    def pair_copy(d, a):
        return pltpu.make_async_remote_copy(
            part(d, a, 1 - core), pbuf.at[d, a], pair_send.at[d, a], pair_recv.at[d, a],
            device_id=(rep, partner), device_id_type=MESH)

    def y_copy(d, a):
        return pltpu.make_async_remote_copy(
            sbuf.at[d - 1, a], rbuf.at[d - 1, a], y_send.at[d - 1, a], y_recv.at[d - 1, a],
            device_id=(rep, 2 * chip_at(d) + core), device_id_type=MESH)

    def ys_copy(d, a):
        return pltpu.make_async_remote_copy(
            sscale.at[d - 1, a], rscale.at[d - 1, a], ys_send.at[d - 1, a], ys_recv.at[d - 1, a],
            device_id=(rep, 2 * chip_at(d) + core), device_id_type=MESH)

    def idx_copy(d):
        return pltpu.make_async_remote_copy(
            idx, gidx.at[d], idx_send.at[d], idx_recv.at[d],
            device_id=(rep_at(d), me), device_id_type=MESH)

    def val_copy(d, a):
        return pltpu.make_async_remote_copy(
            gval.at[0, a], gval.at[d, a], val_send.at[d, a], val_recv.at[d, a],
            device_id=(rep_at(d), me), device_id_type=MESH)

    def each(count, body):
        def step(i, carry):
            body(i)
            return carry
        lax.fori_loop(0, count, step, 0)

    def start_local(a):
        for d in range(1, nq):
            own_copy(d, a).start()
    each(na, start_local)

    barrier = pltpu.get_barrier_semaphore()
    pl.semaphore_signal(barrier, inc=1, device_id=(rep, partner), device_id_type=MESH)
    for d in range(1, nq):
        pl.semaphore_signal(barrier, inc=1, device_id=(rep, 2 * chip_at(d) + core), device_id_type=MESH)
    for d in range(1, nr):
        pl.semaphore_signal(barrier, inc=1, device_id=(rep_at(d), me), device_id_type=MESH)
    pl.semaphore_wait(barrier, nq + nr - 1)

    def start_pairs(a):
        for d in range(1, nq):
            pair_copy(d, a).start()
    each(na, start_pairs)

    def start_rest(a):
        pair_copy(0, a).start()
        own_copy(0, a).start()
        mom_copy(a).start()
    each(na, start_rest)

    span = (2 if ng % 2 == 0 else 1) * WIDE

    def send_sums(a):
        for d in range(1, nq):
            own_copy(d, a).wait()
            pair_copy(d, a).wait_recv()

            def encode(g):
                cols = pl.ds(pl.multiple_of(g * span, span), span)
                total = gbuf[d, a, :, cols].astype(F32) + pbuf[d, a, :, cols].astype(F32)
                top = jnp.maximum(jnp.max(jnp.abs(total), axis=0, keepdims=True), 1e-30)
                sscale[d - 1, a, :, cols] = top * (1.0 / LEVELS)
                sbuf[d - 1, a, :, cols] = jnp.round(total * (LEVELS / top)).astype(jnp.int32).astype(jnp.int16)
            each(width // span, encode)
            y_copy(d, a).start()
            ys_copy(d, a).start()
    each(na, send_sums)

    for d in range(1, nr):
        idx_copy(d).start()
    gidx[0] = idx[...]

    def blocks_of(shape):
        row = lax.broadcasted_iota(jnp.int32, shape, 0) // ORDER
        return row, lax.broadcasted_iota(jnp.int32, shape, 1) // ORDER

    row_block, col_block = blocks_of((WIDE, WIDE))
    for i, (high, low) in enumerate(((rf_high, rf_low), (ri_high, ri_low))):
        tiled = tiled_basis(i == 0)
        wide = jnp.where(row_block == col_block, jnp.concatenate([tiled] * PACK, axis=0), 0.0)
        high[...], low[...] = halves(wide)
    _, col_block = blocks_of((ORDER, WIDE))
    for i, target in enumerate((left_inv, left_fwd)):
        tiled = tiled_basis(i == 0)
        high = tiled.astype(BF16).astype(F32)
        target[...] = jnp.where(col_block == 1, tiled - high, high).astype(BF16)[:, :3 * ORDER]

    for d in range(1, nr):
        idx_copy(d).wait_recv()

    ways = max(w for w in (1, 2, 4) if ng % w == 0)

    def groups(body):
        def some(i):
            gs = [i * ways + w for w in range(ways)]
            body(gs, [pl.ds(pl.multiple_of(g * WIDE, WIDE), WIDE) for g in gs], [pl.ds(g, 1) for g in gs])
        each(ng // ways, some)

    def right_all(xs, w_high, w_low):
        split = [halves(x) for x in xs]
        high = jnp.concatenate([h for h, _ in split], axis=0)
        low = jnp.concatenate([l for _, l in split], axis=0)
        out = mm(high, w_high) + (mm(low, w_high) + mm(high, w_low))
        return [out[w * ORDER:(w + 1) * ORDER] for w in range(len(xs))]

    def decode(pos, val, hots):
        dense = []
        for p, v, columns in zip(pos, val, hots):
            high, low = halves(v)
            hot = hot_rows(p)
            placed = jnp.concatenate(
                [jnp.where(hot, x.astype(F32), 0.0).astype(BF16) for x in (high, low)], axis=0)
            both = mm_nt(placed, columns)
            dense.append(both[:ORDER] + both[ORDER:])
        half = right_all(dense, ri_high[...], ri_low[...])
        return [left_times(left_inv[...], h) for h in half]

    def find_kept(a):
        own_copy(0, a).wait()
        pair_copy(0, a).wait_recv()
        mom_copy(a).wait()
        for d in range(1, nq):
            y_copy(d, a).wait_recv()
            ys_copy(d, a).wait_recv()

        def some(gs, cols, row):
            field = [gbuf[0, a, :, c].astype(F32) + pbuf[0, a, :, c].astype(F32) for c in cols]
            for d in range(1, nq):
                field = [f + rbuf[d - 1, a, :, c].astype(jnp.int32).astype(F32) * rscale[d - 1, a, :, c]
                         for f, c in zip(field, cols)]
            field = [f + MOMENTUM_DECAY * mbuf[rows(a), c] for f, c in zip(field, cols)]
            pos = [gidx[0, a, r, :] for r in row]
            hots = [hot_columns(p, keep) for p in pos]
            half = right_all(field, rf_high[...], rf_low[...])
            coef = [halves(left_times(left_fwd[...], h)) for h in half]
            picked = [mm(jnp.concatenate(c, axis=0), h) for c, h in zip(coef, hots)]
            kept = [jnp.sum(jnp.where(hot_rows(p), x[:ORDER] + x[ORDER:], 0.0), axis=0, keepdims=True)
                    for x, p in zip(picked, pos)]
            for r, k in zip(row, kept):
                gval[0, a, r, :] = k
            for f, x, c in zip(field, decode(pos, kept, hots), cols):
                mbuf[rows(a), c] = f - x
        groups(some)
        for d in range(1, nr):
            val_copy(d, a).start()

    def add_up(a):
        for d in range(1, nr):
            val_copy(d, a).wait_recv()

        def some(gs, cols, row):
            pos = [jnp.concatenate([gidx[d, a, r, :] for d in range(nr)], axis=1) for r in row]
            val = [jnp.concatenate([gval[d, a, r, :] for d in range(nr)], axis=1) for r in row]
            hots = [hot_columns(p, keep) for p in pos]
            for x, c in zip(decode(pos, val, hots), cols):
                ubuf[rows(a), c] = x
        groups(some)

    def step(i):
        @pl.when(i < na)
        def _():
            find_kept(i)

        @pl.when(i > 0)
        def _():
            add_up(i - 1)
    each(na + 1, step)

    def drain(a):
        for d in range(nq):
            pair_copy(d, a).wait_send()
        for d in range(1, nq):
            y_copy(d, a).wait_send()
            ys_copy(d, a).wait_send()
        for d in range(1, nr):
            val_copy(d, a).wait_send()
    each(na, drain)
    for d in range(1, nr):
        idx_copy(d).wait_send()


def local(nr, nf, partial_grads, momentum, freq_index):
    total_rows, width = momentum.shape
    na = total_rows // ORDER
    ng = width // WIDE
    nq = nf // 2
    keep = freq_index.shape[3]
    lanes = PACK * keep
    idx = freq_index.reshape(na, ng, lanes)
    dma = pltpu.SemaphoreType.DMA
    vmem = pl.BlockSpec(memory_space=pltpu.VMEM)
    hbm = pl.BlockSpec(memory_space=pltpu.HBM)
    return pl.pallas_call(
        functools.partial(kernel, nr, nq, na, ng, width, keep),
        out_shape=(
            jax.ShapeDtypeStruct((total_rows, width), F32),
            jax.ShapeDtypeStruct((total_rows, width), F32),
        ),
        in_specs=[hbm, hbm, vmem],
        out_specs=(vmem, vmem),
        scratch_shapes=[
            pltpu.VMEM((WIDE, WIDE), BF16), pltpu.VMEM((WIDE, WIDE), BF16),
            pltpu.VMEM((WIDE, WIDE), BF16), pltpu.VMEM((WIDE, WIDE), BF16),
            pltpu.VMEM((ORDER, 3 * ORDER), BF16), pltpu.VMEM((ORDER, 3 * ORDER), BF16),
            pltpu.VMEM((nq, na, ORDER, width), BF16),
            pltpu.VMEM((nq, na, ORDER, width), BF16),
            pltpu.VMEM((nq - 1, na, ORDER, width), jnp.int16),
            pltpu.VMEM((nq - 1, na, ORDER, width), jnp.int16),
            pltpu.VMEM((nq - 1, na, 1, width), F32),
            pltpu.VMEM((nq - 1, na, 1, width), F32),
            pltpu.VMEM((nr, na, ng, lanes), jnp.int32),
            pltpu.VMEM((nr, na, ng, lanes), F32),
            dma((nq, na)), dma((na,)),
            dma((nq, na)), dma((nq, na)),
            dma((nq - 1, na)), dma((nq - 1, na)), dma((nq - 1, na)), dma((nq - 1, na)),
            dma((nr,)), dma((nr,)), dma((nr, na)), dma((nr, na)),
        ],
        compiler_params=pltpu.CompilerParams(
            collective_id=0, has_side_effects=True, vmem_limit_bytes=43 * 1024 * 1024),
        cost_estimate=pl.CostEstimate(
            flops=20 * 10**9, bytes_accessed=28 * 2**20, transcendentals=0),
    )(partial_grads, momentum, idx)


def solution(mesh):
    return jax.shard_map(
        functools.partial(local, mesh.shape["rep"], mesh.shape["fsdp"]),
        mesh=mesh,
        in_specs=(P(("rep", "fsdp"), None, None), P("rep", "fsdp"), P("rep", None, "fsdp", None)),
        out_specs=(P("rep", "fsdp"), P(None, "fsdp")),
        check_vma=False,
    )
```
